32 devices in a mesh: member: 8 (over y, x, core), tile: 4 (over z).
Axes of the slice: x: 2, y: 2, z: 4, core: 2. Of those that a mesh axis runs over, the one named last changes fastest.
Arguments:
- control: float32 [128, 4, 4, 4096], P('member', 'tile'), may hold values from -6 to 6
- perturbations: float32 [128, 4, 4, 4, 4096], P('member', 'tile'), may hold values from -2 to 2
- diffusivity: float32 [4, 4096], P('tile'), may hold values from 0.02 to 0.24
- flow: float32 [2, 4, 4, 4], P(None, 'tile'), may hold values from 0.02 to 0.22
- observed: float32 [4, 4, 4, 4096], P('tile'), may hold values from -6 to 6
- obs_weight: float32 [4, 4, 4, 4096], P('tile'), may hold values from 0.3 to 3
- neighbour_tile: int32 [4, 4], replicated, may hold values from 0 to 3, as said below
- neighbour_edge: int32 [4, 4], replicated, may hold values from 0 to 3
- departure: int32 [4, 4, 64], replicated, may hold values from 0 to 63, as said below
Outputs:
- gradient: float32 [128, 4, 4, 4096], P('member', 'tile')
The draws below stay inside these ranges and needn't reach their ends.
Inputs may be any that keep to these rules, and one draw needn't show every extreme that they name: `neighbour_tile`: edges are glued in pairs: if edge e of tile t meets edge e2 of tile u, then edge e2 of tile u meets edge e of tile t. `departure`: each row is 0 to 63 in order or reversed, the same way for both edges of a glued pair.
All inputs are finite; a program needn't handle non-finite values.
Results may differ from the reference program's by a relative error of at most 0.0001.
Values sent between devices are 32-bit elements; how exact they have to be, the bound alone decides.
A program may use at most 128 MiB of HBM per device.

```python
import math
import jax
import jax.numpy as jnp
from jax import lax

S = 64
V = 4
L = 4
SWEEPS = 8
STEPS = 2
MEMBERS = 128
TILES = 4
CELLS = 4096


def glued_edges(key):
    slot_count = 4 * TILES
    shuffled = jax.random.permutation(jax.random.fold_in(key, 101), slot_count).astype(jnp.int32)
    firsts = shuffled[0::2]
    seconds = shuffled[1::2]
    partner = jnp.zeros((slot_count,), jnp.int32).at[firsts].set(seconds).at[seconds].set(firsts)
    flip_bits = jax.random.randint(jax.random.fold_in(key, 202), (slot_count // 2,), 0, 2).astype(jnp.int32)
    flipped = jnp.zeros((slot_count,), jnp.int32).at[firsts].set(flip_bits).at[seconds].set(flip_bits)
    return (partner, flipped)


def draw_neighbour_tile(key, part):
    partner, flipped = glued_edges(key)
    return (partner // 4).reshape(TILES, 4)


def draw_neighbour_edge(key, part):
    partner, flipped = glued_edges(key)
    return (partner % 4).reshape(TILES, 4)


def draw_departure(key, part):
    partner, flipped = glued_edges(key)
    positions = jnp.arange(S, dtype=jnp.int32)
    indices = jnp.where(flipped[:, None] == 1, S - 1 - positions[None, :], positions[None, :])
    return indices.reshape(TILES, 4, S).astype(jnp.int32)


def block_levels(own_key, shape, pieces, low, largest):
    gain = 1.0
    for position, blocks in pieces:
        draws = jax.random.uniform(jax.random.fold_in(jax.random.fold_in(own_key, 6), position), (blocks,), jnp.float32, low / len(pieces), largest / len(pieces))
        gain = gain * jnp.repeat(jnp.exp(draws), shape[position] // blocks).reshape((-1,) + (1,) * (len(shape) - 1 - position))
    return gain


def noise(key, shape, spread, most, pieces=(), kind=jnp.bfloat16):
    array = spread * jax.random.normal(key, shape, jnp.float32)
    if pieces:
        array = array * block_levels(key, shape, pieces, -0.22, 0.18)
    return jnp.clip(array, -most, most).astype(kind)


def setup_inputs(seed: int = 0) -> dict:
    streams_of = jax.random.split(jax.random.key(seed), 10)
    return {
        "control": noise(streams_of[0], (MEMBERS, TILES, L, CELLS), 1.0, 6.0, ((0, 8), (1, 4)), jnp.float32),
        "perturbations": noise(streams_of[1], (MEMBERS, TILES, V, L, CELLS), (MEMBERS // 16) ** -0.5, 2.0, ((0, 8), (1, 4)), jnp.float32),
        "diffusivity": jnp.clip(jnp.exp(math.log(0.24) - 2.4849066 * jax.random.uniform(streams_of[2], (TILES, CELLS), jnp.float32) ** block_levels(streams_of[2], (TILES, CELLS), ((0, 4),), -0.2, 0.2)), 0.02, 0.24),
        "flow": jnp.clip(0.02 + 0.2 * jax.random.uniform(streams_of[3], (STEPS, TILES, L, 4), jnp.float32) ** block_levels(streams_of[3], (STEPS, TILES, L, 4), ((1, 4),), -0.2, 0.2), 0.02, 0.22),
        "observed": noise(streams_of[4], (TILES, V, L, CELLS), 1.0, 6.0, ((0, 4),), jnp.float32),
        "obs_weight": jnp.clip(jnp.exp(math.log(3.0) - 2.3025851 * jax.random.uniform(streams_of[5], (TILES, V, L, CELLS), jnp.float32) ** block_levels(streams_of[5], (TILES, V, L, CELLS), ((0, 4),), -0.2, 0.2)), 0.3, 3.0),
        "neighbour_tile": draw_neighbour_tile(jax.random.fold_in(streams_of[9], 71), 0),
        "neighbour_edge": draw_neighbour_edge(jax.random.fold_in(streams_of[9], 71), 0),
        "departure": draw_departure(jax.random.fold_in(streams_of[9], 71), 0),
    }


PRECISE = lax.Precision.HIGHEST


def edge_strips(values):
    return jnp.stack([values[..., 0, :], values[..., -1, :], values[..., :, 0], values[..., :, -1]], axis=2)


def combine(values, ghosts, factors):
    before_rows = jnp.concatenate([ghosts[:, :, 0, :, None, :], values[..., :-1, :]], axis=-2)
    after_rows = jnp.concatenate([values[..., 1:, :], ghosts[:, :, 1, :, None, :]], axis=-2)
    before_cols = jnp.concatenate([ghosts[:, :, 2, :, :, None], values[..., :, :-1]], axis=-1)
    after_cols = jnp.concatenate([values[..., :, 1:], ghosts[:, :, 3, :, :, None]], axis=-1)
    return (factors[0] * values + factors[1] * before_rows + factors[2] * after_rows
            + factors[3] * before_cols + factors[4] * after_cols)


def spread_back(values, factors):
    parts = [factors[1 + which] * values for which in range(4)]
    zero_row = jnp.zeros_like(values[..., :1, :])
    zero_col = jnp.zeros_like(values[..., :, :1])
    inner = factors[0] * values
    inner = inner + jnp.concatenate([parts[0][..., 1:, :], zero_row], axis=-2)
    inner = inner + jnp.concatenate([zero_row, parts[1][..., :-1, :]], axis=-2)
    inner = inner + jnp.concatenate([parts[2][..., :, 1:], zero_col], axis=-1)
    inner = inner + jnp.concatenate([zero_col, parts[3][..., :, :-1]], axis=-1)
    outward = jnp.stack([parts[0][..., 0, :], parts[1][..., -1, :], parts[2][..., :, 0], parts[3][..., :, -1]], axis=2)
    return inner, outward


def add_edges(inner, incoming):
    zero_rows = jnp.zeros_like(inner[..., 1:, :])
    zero_cols = jnp.zeros_like(inner[..., :, 1:])
    inner = inner + jnp.concatenate([incoming[:, :, 0, :, None, :], zero_rows], axis=-2)
    inner = inner + jnp.concatenate([zero_rows, incoming[:, :, 1, :, None, :]], axis=-2)
    inner = inner + jnp.concatenate([incoming[:, :, 2, :, :, None], zero_cols], axis=-1)
    inner = inner + jnp.concatenate([zero_cols, incoming[:, :, 3, :, :, None]], axis=-1)
    return inner


def forward_map(values, factors, tables):
    neighbour_tile, neighbour_edge, permute = tables
    strips = edge_strips(values)
    picked = strips[:, neighbour_tile, neighbour_edge]
    ghosts = jnp.einsum("pteqm,tekm->pteqk", picked, permute, precision=PRECISE)
    return combine(values, ghosts, factors)


def adjoint_map(values, factors, tables):
    neighbour_tile, neighbour_edge, permute = tables
    inner, outward = spread_back(values, factors)
    sent = jnp.einsum("pteqk,tekm->pteqm", outward, permute, precision=PRECISE)
    incoming = jnp.zeros_like(sent).at[:, neighbour_tile, neighbour_edge].add(sent)
    return add_edges(inner, incoming)


def reference(control, perturbations, diffusivity, flow, observed, obs_weight, neighbour_tile, neighbour_edge, departure):
    permute = (departure[..., None] == jnp.arange(S, dtype=jnp.int32)).astype(jnp.float32)
    tables = (neighbour_tile, neighbour_edge, permute)
    rate = diffusivity.reshape(1, TILES, 1, S, S)
    smooth_factors = (1.0 - 4.0 * rate, rate, rate, rate, rate)

    def smooth(values, adjoint):
        grid = values.reshape(1, TILES, L, S, S)
        for repeat in range(SWEEPS):
            if adjoint:
                grid = adjoint_map(grid, smooth_factors, tables)
            else:
                grid = forward_map(grid, smooth_factors, tables)
        return grid[0]

    def accumulate(running, member_pair):
        member_control, member_pert = member_pair
        smoothed = smooth(member_control, False)
        return running + member_pert.reshape(TILES, V, L, S, S) * smoothed[:, None], None

    increment = lax.scan(accumulate, jnp.zeros((TILES, V, L, S, S), jnp.float32), (control, perturbations))[0]

    def flow_factors(section):
        speeds = jnp.tile(flow[section], (1, V, 1))[None, :, :, :, None, None]
        return (1.0 - jnp.sum(speeds, axis=3), speeds[:, :, :, 0], speeds[:, :, :, 1],
                speeds[:, :, :, 2], speeds[:, :, :, 3])

    state = increment.reshape(1, TILES, V * L, S, S)
    for section in range(STEPS):
        state = forward_map(state, flow_factors(section), tables)
    misfit = obs_weight.reshape(1, TILES, V * L, S, S) * (state - observed.reshape(1, TILES, V * L, S, S))
    for section in reversed(range(STEPS)):
        misfit = adjoint_map(misfit, flow_factors(section), tables)
    sensitivity = misfit.reshape(TILES, V, L, S * S)

    def gradient_of(member_pair):
        member_control, member_pert = member_pair
        projected = jnp.sum(member_pert * sensitivity, axis=1)
        return member_control + smooth(projected, True).reshape(TILES, L, S * S)

    return lax.map(gradient_of, (control, perturbations))
```

```python
import functools

import jax
import jax.numpy as jnp
from jax import lax
from jax.experimental import pallas as pl
from jax.experimental.pallas import tpu as pltpu
from jax.sharding import PartitionSpec as P

SWEEPS = 8
ROWS = 8
MESH = pl.DeviceIdType.MESH
VMEM_LIMIT = 40 * 1024 * 1024


def exchange_kernel(tcount, n_scatter, n_gather, *refs):
    count = n_scatter + n_gather
    ins, outs = refs[:count], refs[count : 2 * count]
    send_sem, recv_sem, own_sem = refs[2 * count :]
    me = lax.axis_index("tile")
    barrier = pltpu.get_barrier_semaphore()
    for step in range(1, tcount):
        pl.semaphore_signal(
            barrier, inc=1, device_id={"tile": lax.rem(me + step, tcount)}, device_id_type=MESH
        )
    pl.semaphore_wait(barrier, tcount - 1)
    copies = []
    order = list(range(n_scatter, count)) + list(range(n_scatter))
    for which in order:
        for step in range(1, tcount):
            peer = lax.rem(me + step, tcount)
            block = ins[which].at[peer] if which < n_scatter else ins[which]
            copy = pltpu.make_async_remote_copy(
                src_ref=block,
                dst_ref=outs[which].at[me],
                send_sem=send_sem.at[which, step - 1],
                recv_sem=recv_sem.at[which, step - 1],
                device_id={"tile": peer},
                device_id_type=MESH,
            )
            copy.start()
            copies.append(copy)
    owns = []
    for which in order:
        block = ins[which].at[me] if which < n_scatter else ins[which]
        copy = pltpu.make_async_copy(block, outs[which].at[me], own_sem.at[which])
        copy.start()
        owns.append(copy)
    for copy in owns:
        copy.wait()
    for copy in copies:
        copy.wait()


def exchange(tcount, collective_id, scatter, gather=()):
    arrays = list(scatter) + list(gather)
    shapes = [jax.ShapeDtypeStruct(a.shape, a.dtype) for a in scatter]
    shapes += [jax.ShapeDtypeStruct((tcount,) + a.shape, a.dtype) for a in gather]
    sems = (len(arrays), max(tcount - 1, 1))
    return pl.pallas_call(
        functools.partial(exchange_kernel, tcount, len(scatter), len(gather)),
        out_shape=shapes,
        in_specs=[pl.BlockSpec(memory_space=pl.ANY)] * len(arrays),
        out_specs=[pl.BlockSpec(memory_space=pl.ANY)] * len(arrays),
        scratch_shapes=[
            pltpu.SemaphoreType.DMA(sems),
            pltpu.SemaphoreType.DMA(sems),
            pltpu.SemaphoreType.DMA((len(arrays),)),
        ],
        compiler_params=pltpu.CompilerParams(collective_id=collective_id, has_side_effects=True),
    )(*arrays)


def reduce_kernel(mcount, tcount, part_ref, out_ref, landed, msend, mrecv, tsend, trecv):
    mine = lax.axis_index("member")
    here = lax.axis_index("tile")
    barrier = pltpu.get_barrier_semaphore()
    for step in range(1, mcount):
        pl.semaphore_signal(
            barrier, inc=1, device_id={"member": lax.rem(mine + step, mcount)}, device_id_type=MESH
        )
    for step in range(1, tcount):
        pl.semaphore_signal(
            barrier, inc=1, device_id={"tile": lax.rem(here + step, tcount)}, device_id_type=MESH
        )
    pl.semaphore_wait(barrier, mcount + tcount - 2)
    copies = []
    for step in range(1, mcount):
        peer = lax.rem(mine + step, mcount)
        copy = pltpu.make_async_remote_copy(
            src_ref=part_ref.at[peer],
            dst_ref=landed.at[step - 1],
            send_sem=msend.at[step - 1],
            recv_sem=mrecv.at[step - 1],
            device_id={"member": peer},
            device_id_type=MESH,
        )
        copy.start()
        copies.append(copy)
    for copy in copies:
        copy.wait()
    total = part_ref[mine]
    for step in range(1, mcount):
        total = total + landed[step - 1]
    out_ref[here] = total
    copies = []
    for step in range(1, tcount):
        copy = pltpu.make_async_remote_copy(
            src_ref=out_ref.at[here],
            dst_ref=out_ref.at[here],
            send_sem=tsend.at[step - 1],
            recv_sem=trecv.at[step - 1],
            device_id={"tile": lax.rem(here + step, tcount)},
            device_id_type=MESH,
        )
        copy.start()
        copies.append(copy)
    for copy in copies:
        copy.wait()


def reduce_fields(part, mcount, tcount, collective_id):
    block = part.shape[1:]
    return pl.pallas_call(
        functools.partial(reduce_kernel, mcount, tcount),
        out_shape=jax.ShapeDtypeStruct((tcount,) + block, jnp.float32),
        in_specs=[pl.BlockSpec(memory_space=pltpu.VMEM)],
        out_specs=pl.BlockSpec(memory_space=pltpu.VMEM),
        scratch_shapes=[
            pltpu.VMEM((max(mcount - 1, 1),) + block, jnp.float32),
            pltpu.SemaphoreType.DMA((max(mcount - 1, 1),)),
            pltpu.SemaphoreType.DMA((max(mcount - 1, 1),)),
            pltpu.SemaphoreType.DMA((max(tcount - 1, 1),)),
            pltpu.SemaphoreType.DMA((max(tcount - 1, 1),)),
        ],
        compiler_params=pltpu.CompilerParams(
            collective_id=collective_id, has_side_effects=True, vmem_limit_bytes=VMEM_LIMIT
        ),
    )(part)


def spread_kernel(mcount, own_ref, out_ref, msend, mrecv):
    mine = lax.axis_index("member")
    here = lax.axis_index("tile")
    barrier = pltpu.get_barrier_semaphore()
    for step in range(1, mcount):
        pl.semaphore_signal(
            barrier, inc=1, device_id={"member": lax.rem(mine + step, mcount)}, device_id_type=MESH
        )
    pl.semaphore_wait(barrier, mcount - 1)
    copies = []
    for step in range(1, mcount):
        copy = pltpu.make_async_remote_copy(
            src_ref=own_ref.at[here],
            dst_ref=out_ref.at[mine],
            send_sem=msend.at[step - 1],
            recv_sem=mrecv.at[step - 1],
            device_id={"member": lax.rem(mine + step, mcount)},
            device_id_type=MESH,
        )
        copy.start()
        copies.append(copy)
    out_ref[mine] = own_ref[here]
    for copy in copies:
        copy.wait()


def spread_fields(fields, mcount, collective_id):
    return pl.pallas_call(
        functools.partial(spread_kernel, mcount),
        out_shape=jax.ShapeDtypeStruct((mcount,) + fields.shape[1:], jnp.float32),
        in_specs=[pl.BlockSpec(memory_space=pltpu.VMEM)],
        out_specs=pl.BlockSpec(memory_space=pltpu.VMEM),
        scratch_shapes=[
            pltpu.SemaphoreType.DMA((max(mcount - 1, 1),)),
            pltpu.SemaphoreType.DMA((max(mcount - 1, 1),)),
        ],
        compiler_params=pltpu.CompilerParams(
            collective_id=collective_id, has_side_effects=True, vmem_limit_bytes=VMEM_LIMIT
        ),
    )(fields)


def lane_grid(lanes):
    return lax.broadcasted_iota(jnp.int32, (ROWS, lanes), 1)


def lane_of(edge, position, side):
    lanes = 2 * side
    column = side * (position & 1) + (position - (position & 1))
    column = column + jnp.where(edge == 3, side - 1, 0)
    column = jnp.where(column >= lanes, column - lanes, column)
    return jnp.where(edge < 2, position + side * edge, column)


def fill_index(nedge_ref, depart_ref, idx, tile, side):
    lanes = 2 * side
    lane = lane_grid(lanes)

    def source(pair, first, position):
        edge = jnp.where(first, nedge_ref[tile, pair], nedge_ref[tile, pair + 1])
        flip = jnp.where(first, depart_ref[tile, pair, 0], depart_ref[tile, pair + 1, 0])
        position = jnp.where(flip != 0, side - 1 - position, position)
        return lane_of(edge, position, side)

    low = lane < side
    idx[2 * tile + 1] = source(0, low, jnp.where(low, lane, lane - side))
    even = (lane & 1) == 0
    base = jnp.where(even, lane, (lane + side + 1) & (lanes - 1))
    upper = base >= side
    position = jnp.where(upper, base - side + 1, base)
    idx[2 * tile] = source(2, even, position)


def slot_of(ntile_ref, nedge_ref, tile, edge):
    return 2 * ntile_ref[tile, edge] + jnp.where(nedge_ref[tile, edge] < 2, 1, 0)


def pick(values, index):
    return jnp.take_along_axis(values, index, axis=1, mode="promise_in_bounds")


def column_part(piece, j, corner, lanes):
    kept = jnp.where(corner, piece, 0.0)
    return kept if j == 0 else pltpu.roll(kept, 2 * j, 1)


def store_edges(es, phase, tile, columns, first, last, low):
    while len(columns) > 1:
        columns = [sum(columns[i : i + 2]) for i in range(0, len(columns), 2)]
    es[phase, 2 * tile] = columns[0]
    es[phase, 2 * tile + 1] = jnp.where(low, first, last)


def masks(side):
    lanes = 2 * side
    lane = lane_grid(lanes)
    low = lane < side
    left = (lane & (side - 1)) == 0
    right = (lane & (side - 1)) == side - 1
    return low, left, right, left | right, (lane & 1) == 0


def localise_kernel(adjoint, side, ntile_ref, nedge_ref, depart_ref, x_ref, d_ref, out_ref, xs, es, idx):
    tcount, pieces, _, lanes = xs.shape
    low, left, right, corner, even = masks(side)

    def load(tile, carry):
        fill_index(nedge_ref, depart_ref, idx, tile, side)
        columns = []
        for j in range(pieces):
            cells = slice(j * lanes, (j + 1) * lanes)
            x = jnp.concatenate([x_ref[tile, m, :, cells] for m in range(x_ref.shape[1])], axis=0)
            if adjoint:
                x = x * d_ref[tile, :, cells]
            xs[tile, j] = x
            columns.append(column_part(x, j, corner, lanes))
            if j == 0:
                first = x
        store_edges(es, 0, tile, columns, first, x, low)
        return carry

    lax.fori_loop(0, tcount, load, 0)

    def sweep(repeat, carry):
        phase = lax.rem(repeat, 2)

        def one(tile, inner):
            slots = [slot_of(ntile_ref, nedge_ref, tile, edge) for edge in range(4)]
            got = [es[phase, slot] for slot in slots]
            row_idx, col_idx = idx[2 * tile + 1], idx[2 * tile]
            rows = jnp.where(low, pick(got[0], row_idx), pick(got[1], row_idx))
            cols = jnp.where(even, pick(got[2], col_idx), pick(got[3], col_idx))
            x = xs[tile, 0]
            before, here = rows, pltpu.roll(x, side, 1)
            columns = []
            for j in range(pieces):
                if j + 1 < pieces:
                    after_x = xs[tile, j + 1]
                    after = pltpu.roll(after_x, side, 1)
                else:
                    after_x, after = None, rows
                ghost = cols if j == 0 else pltpu.roll(cols, lanes - 2 * j, 1)
                total = here + jnp.where(low, before, after)
                total = total + jnp.where(left, ghost, pltpu.roll(x, 1, 1))
                total = total + jnp.where(right, ghost, pltpu.roll(x, lanes - 1, 1))
                rate = d_ref[tile, :, j * lanes : (j + 1) * lanes]
                new = x + rate * (total - 4.0 * x)
                xs[tile, j] = new
                columns.append(column_part(new, j, corner, lanes))
                if j == 0:
                    first = new
                x, before, here = after_x, here, after
            store_edges(es, 1 - phase, tile, columns, first, new, low)
            return inner

        return lax.fori_loop(0, tcount, one, carry)

    lax.fori_loop(0, SWEEPS, sweep, 0)

    def store(tile, carry):
        depth = x_ref.shape[2]
        for j in range(pieces):
            cells = slice(j * lanes, (j + 1) * lanes)
            x = xs[tile, j]
            if adjoint:
                x = x / d_ref[tile, :, cells]
            for m in range(x_ref.shape[1]):
                out_ref[tile, m, :, cells] = x[m * depth : (m + 1) * depth]
        return carry

    lax.fori_loop(0, tcount, store, 0)


def localise(values, rate, tables, side, adjoint):
    tcount, members, depth, cells = values.shape
    lanes = 2 * side
    pair = ROWS // depth
    block = pl.BlockSpec((tcount, pair, depth, cells), lambda i: (0, i, 0, 0))
    smem = pl.BlockSpec(memory_space=pltpu.SMEM)
    return pl.pallas_call(
        functools.partial(localise_kernel, adjoint, side),
        out_shape=jax.ShapeDtypeStruct(values.shape, jnp.float32),
        grid=(members // pair,),
        in_specs=[smem, smem, smem, block, pl.BlockSpec(rate.shape, lambda i: (0, 0, 0))],
        out_specs=block,
        scratch_shapes=[
            pltpu.VMEM((tcount, cells // lanes, ROWS, lanes), jnp.float32),
            pltpu.VMEM((2, 2 * tcount, ROWS, lanes), jnp.float32),
            pltpu.VMEM((2 * tcount, ROWS, lanes), jnp.int32),
        ],
        compiler_params=pltpu.CompilerParams(vmem_limit_bytes=VMEM_LIMIT),
    )(*tables, values, rate)


def transport_kernel(
    side, depth, mine_ref, ntile_ref, nedge_ref, depart_ref, flow_ref,
    x_ref, observed_ref, weight_ref, out_ref, xs, es, idx, coef,
):
    tcount, pieces, _, lanes = xs.shape
    steps = flow_ref.shape[1]
    fields = x_ref.shape[1]
    low, left, right, corner, even = masks(side)
    row = lax.broadcasted_iota(jnp.int32, (ROWS, lanes), 0)
    level = lax.rem(mine_ref[0] * fields + lax.rem(row, fields), depth)

    def wide(ref, tile, cells):
        return jnp.concatenate([ref[tile, :, cells]] * (ROWS // fields), axis=0)

    def load(tile, carry):
        fill_index(nedge_ref, depart_ref, idx, tile, side)
        for step in range(steps):
            rest = jnp.ones((ROWS, lanes), jnp.float32)
            for way in range(4):
                speed = jnp.zeros((ROWS, lanes), jnp.float32)
                for at in range(depth):
                    speed = jnp.where(level == at, flow_ref[tile, step, at, way], speed)
                coef[step, tile, way] = speed
                rest = rest - speed
            coef[step, tile, 4] = rest
        columns = []
        for j in range(pieces):
            x = wide(x_ref, tile, slice(j * lanes, (j + 1) * lanes))
            xs[tile, j] = x
            columns.append(column_part(x, j, corner, lanes))
            if j == 0:
                first = x
        store_edges(es, 0, tile, columns, first, x, low)
        return carry

    lax.fori_loop(0, tcount, load, 0)

    turns = [(s, False) for s in range(steps)] + [(s, True) for s in reversed(range(steps))]
    for turn, (step, adjoint) in enumerate(turns):

        def one(tile, carry, turn=turn, step=step, adjoint=adjoint):
            picked = []
            for edge in range(4):
                values = es[turn % 2, slot_of(ntile_ref, nedge_ref, tile, edge)]
                values = pick(values, idx[2 * tile + (1 if edge < 2 else 0)])
                if adjoint:
                    scale = coef[step, ntile_ref[tile, edge], nedge_ref[tile, edge]]
                else:
                    scale = coef[step, tile, edge]
                picked.append(values * scale)
            rows = jnp.where(low, picked[0], picked[1])
            cols = jnp.where(even, picked[2], picked[3])
            speeds = [coef[step, tile, way] for way in range(4)]
            if adjoint:
                speeds = [speeds[1], speeds[0], speeds[3], speeds[2]]
            rest = coef[step, tile, 4]
            x = xs[tile, 0]
            before, here = None, pltpu.roll(x, side, 1)
            columns = []
            for j in range(pieces):
                if j + 1 < pieces:
                    after_x = xs[tile, j + 1]
                    after = pltpu.roll(after_x, side, 1)
                    down = speeds[1] * jnp.where(low, here, after)
                else:
                    after_x, after = None, None
                    down = jnp.where(low, speeds[1] * here, rows)
                if j == 0:
                    up = jnp.where(low, rows, speeds[0] * here)
                else:
                    up = speeds[0] * jnp.where(low, before, here)
                ghost = cols if j == 0 else pltpu.roll(cols, lanes - 2 * j, 1)
                new = rest * x + up + down
                new = new + jnp.where(left, ghost, speeds[2] * pltpu.roll(x, 1, 1))
                new = new + jnp.where(right, ghost, speeds[3] * pltpu.roll(x, lanes - 1, 1))
                cells = slice(j * lanes, (j + 1) * lanes)
                if turn == steps - 1:
                    new = wide(weight_ref, tile, cells) * (new - wide(observed_ref, tile, cells))
                if turn == len(turns) - 1:
                    out_ref[tile, :, cells] = new[:fields]
                else:
                    xs[tile, j] = new
                    columns.append(column_part(new, j, corner, lanes))
                if j == 0:
                    first = new
                x, before, here = after_x, here, after
            if turn < len(turns) - 1:
                store_edges(es, 1 - turn % 2, tile, columns, first, new, low)
            return carry

        lax.fori_loop(0, tcount, one, 0)


def transport(states, observed, weight, flow, tables, mine, side, depth):
    tcount, fields, cells = states.shape
    lanes = 2 * side
    smem = pl.BlockSpec(memory_space=pltpu.SMEM)
    vmem = pl.BlockSpec(memory_space=pltpu.VMEM)
    return pl.pallas_call(
        functools.partial(transport_kernel, side, depth),
        out_shape=jax.ShapeDtypeStruct(states.shape, jnp.float32),
        in_specs=[smem] * 5 + [vmem] * 3,
        out_specs=vmem,
        scratch_shapes=[
            pltpu.VMEM((tcount, cells // lanes, ROWS, lanes), jnp.float32),
            pltpu.VMEM((2, 2 * tcount, ROWS, lanes), jnp.float32),
            pltpu.VMEM((2 * tcount, ROWS, lanes), jnp.int32),
            pltpu.VMEM((flow.shape[1], tcount, 5, ROWS, lanes), jnp.float32),
        ],
        compiler_params=pltpu.CompilerParams(vmem_limit_bytes=VMEM_LIMIT),
    )(mine, *tables, flow, states, observed, weight)


def body(
    mcount,
    tcount,
    control,
    perturbations,
    diffusivity,
    flow,
    observed,
    obs_weight,
    neighbour_tile,
    neighbour_edge,
    departure,
):
    members, _, depth, cells = control.shape
    kinds = perturbations.shape[2]
    side = departure.shape[-1]
    share = kinds * depth // mcount
    mine = lax.axis_index("member")
    tables = (neighbour_tile, neighbour_edge, departure)

    def own_fields(values):
        grouped = values.reshape(mcount, share, cells)
        return lax.dynamic_index_in_dim(grouped, mine, 0, keepdims=False)

    grouped = (tcount, members // tcount, depth, cells)
    spread, rate, flows, target, weight = exchange(
        tcount, 1, [control.reshape(grouped)],
        [diffusivity, flow[:, 0], own_fields(observed), own_fields(obs_weight)],
    )
    mixed = localise(spread, rate, tables, side, False)
    smoothed = exchange(tcount, 2, [mixed])[0].reshape(members, depth, cells)
    part = jnp.sum(perturbations[:, 0] * smoothed[:, None], axis=0)
    states = reduce_fields(part.reshape(mcount, share, cells), mcount, tcount, 3)
    sensitivity = transport(states, target, weight, flows, tables, mine.reshape(1), side, depth)
    sensitivity = spread_fields(sensitivity, mcount, 4).reshape(kinds, depth, cells)
    projected = jnp.sum(perturbations[:, 0] * sensitivity[None], axis=1)
    mixed = localise(exchange(tcount, 5, [projected.reshape(grouped)])[0], rate, tables, side, True)
    return control + exchange(tcount, 6, [mixed])[0].reshape(control.shape)


def solution(mesh):
    in_specs = (
        P("member", "tile", None, None),
        P("member", "tile", None, None, None),
        P("tile", None),
        P(None, "tile", None, None),
        P("tile", None, None, None),
        P("tile", None, None, None),
        P(),
        P(),
        P(),
    )
    out_specs = P("member", "tile", None, None)
    run = functools.partial(body, mesh.shape["member"], mesh.shape["tile"])
    return jax.shard_map(run, mesh=mesh, in_specs=in_specs, out_specs=out_specs, check_vma=False)
```

```python
import functools

import jax
import jax.numpy as jnp
from jax import lax
from jax.experimental import pallas as pl
from jax.experimental.pallas import tpu as pltpu
from jax.sharding import PartitionSpec as P

SWEEPS = 8
ROWS = 8
MESH = pl.DeviceIdType.MESH
VMEM_LIMIT = 40 * 1024 * 1024


def reduce_kernel(mcount, tcount, part_ref, out_ref, landed, msend, mrecv, tsend, trecv):
    mine = lax.axis_index("member")
    here = lax.axis_index("tile")
    barrier = pltpu.get_barrier_semaphore()
    for step in range(1, mcount):
        pl.semaphore_signal(
            barrier, inc=1, device_id={"member": lax.rem(mine + step, mcount)}, device_id_type=MESH
        )
    for step in range(1, tcount):
        pl.semaphore_signal(
            barrier, inc=1, device_id={"tile": lax.rem(here + step, tcount)}, device_id_type=MESH
        )
    pl.semaphore_wait(barrier, mcount + tcount - 2)
    copies = []
    for step in range(1, mcount):
        peer = lax.rem(mine + step, mcount)
        copy = pltpu.make_async_remote_copy(
            src_ref=part_ref.at[peer],
            dst_ref=landed.at[step - 1],
            send_sem=msend.at[step - 1],
            recv_sem=mrecv.at[step - 1],
            device_id={"member": peer},
            device_id_type=MESH,
        )
        copy.start()
        copies.append(copy)
    for copy in copies:
        copy.wait()
    total = part_ref[mine]
    for step in range(1, mcount):
        total = total + landed[step - 1]
    out_ref[here] = total
    copies = []
    for step in range(1, tcount):
        copy = pltpu.make_async_remote_copy(
            src_ref=out_ref.at[here],
            dst_ref=out_ref.at[here],
            send_sem=tsend.at[step - 1],
            recv_sem=trecv.at[step - 1],
            device_id={"tile": lax.rem(here + step, tcount)},
            device_id_type=MESH,
        )
        copy.start()
        copies.append(copy)
    for copy in copies:
        copy.wait()


def reduce_fields(part, mcount, tcount, collective_id):
    block = part.shape[1:]
    return pl.pallas_call(
        functools.partial(reduce_kernel, mcount, tcount),
        out_shape=jax.ShapeDtypeStruct((tcount,) + block, jnp.float32),
        in_specs=[pl.BlockSpec(memory_space=pltpu.VMEM)],
        out_specs=pl.BlockSpec(memory_space=pltpu.VMEM),
        scratch_shapes=[
            pltpu.VMEM((max(mcount - 1, 1),) + block, jnp.float32),
            pltpu.SemaphoreType.DMA((max(mcount - 1, 1),)),
            pltpu.SemaphoreType.DMA((max(mcount - 1, 1),)),
            pltpu.SemaphoreType.DMA((max(tcount - 1, 1),)),
            pltpu.SemaphoreType.DMA((max(tcount - 1, 1),)),
        ],
        compiler_params=pltpu.CompilerParams(
            collective_id=collective_id, has_side_effects=True, vmem_limit_bytes=VMEM_LIMIT
        ),
    )(part)


def spread_kernel(mcount, own_ref, out_ref, msend, mrecv):
    mine = lax.axis_index("member")
    here = lax.axis_index("tile")
    barrier = pltpu.get_barrier_semaphore()
    for step in range(1, mcount):
        pl.semaphore_signal(
            barrier, inc=1, device_id={"member": lax.rem(mine + step, mcount)}, device_id_type=MESH
        )
    pl.semaphore_wait(barrier, mcount - 1)
    copies = []
    for step in range(1, mcount):
        copy = pltpu.make_async_remote_copy(
            src_ref=own_ref.at[here],
            dst_ref=out_ref.at[mine],
            send_sem=msend.at[step - 1],
            recv_sem=mrecv.at[step - 1],
            device_id={"member": lax.rem(mine + step, mcount)},
            device_id_type=MESH,
        )
        copy.start()
        copies.append(copy)
    out_ref[mine] = own_ref[here]
    for copy in copies:
        copy.wait()


def spread_fields(fields, mcount, collective_id):
    return pl.pallas_call(
        functools.partial(spread_kernel, mcount),
        out_shape=jax.ShapeDtypeStruct((mcount,) + fields.shape[1:], jnp.float32),
        in_specs=[pl.BlockSpec(memory_space=pltpu.VMEM)],
        out_specs=pl.BlockSpec(memory_space=pltpu.VMEM),
        scratch_shapes=[
            pltpu.SemaphoreType.DMA((max(mcount - 1, 1),)),
            pltpu.SemaphoreType.DMA((max(mcount - 1, 1),)),
        ],
        compiler_params=pltpu.CompilerParams(
            collective_id=collective_id, has_side_effects=True, vmem_limit_bytes=VMEM_LIMIT
        ),
    )(fields)


def lane_grid(lanes):
    return lax.broadcasted_iota(jnp.int32, (ROWS, lanes), 1)


def lane_of(edge, position, side):
    lanes = 2 * side
    column = side * (position & 1) + (position - (position & 1))
    column = column + jnp.where(edge == 3, side - 1, 0)
    column = jnp.where(column >= lanes, column - lanes, column)
    return jnp.where(edge < 2, position + side * edge, column)


def fill_index(nedge_ref, depart_ref, idx, tile, side):
    lanes = 2 * side
    lane = lane_grid(lanes)

    def source(pair, first, position):
        edge = jnp.where(first, nedge_ref[tile, pair], nedge_ref[tile, pair + 1])
        flip = jnp.where(first, depart_ref[tile, pair, 0], depart_ref[tile, pair + 1, 0])
        position = jnp.where(flip != 0, side - 1 - position, position)
        return lane_of(edge, position, side)

    low = lane < side
    idx[2 * tile + 1] = source(0, low, jnp.where(low, lane, lane - side))
    even = (lane & 1) == 0
    base = jnp.where(even, lane, (lane + side + 1) & (lanes - 1))
    upper = base >= side
    position = jnp.where(upper, base - side + 1, base)
    idx[2 * tile] = source(2, even, position)


def slot_of(ntile_ref, nedge_ref, tile, edge):
    return 2 * ntile_ref[tile, edge] + jnp.where(nedge_ref[tile, edge] < 2, 1, 0)


def pick(values, index):
    return jnp.take_along_axis(values, index, axis=1, mode="promise_in_bounds")


def column_part(piece, j, corner, lanes):
    kept = jnp.where(corner, piece, 0.0)
    return kept if j == 0 else pltpu.roll(kept, 2 * j, 1)


def store_edges(es, tile, columns, first, last, low):
    while len(columns) > 1:
        columns = [sum(columns[i : i + 2]) for i in range(0, len(columns), 2)]
    es[2 * tile] = columns[0]
    es[2 * tile + 1] = jnp.where(low, first, last)


def masks(side):
    lanes = 2 * side
    lane = lane_grid(lanes)
    low = lane < side
    left = (lane & (side - 1)) == 0
    right = (lane & (side - 1)) == side - 1
    return low, left, right, left | right, (lane & 1) == 0


def over_tiles(tcount, visit):
    group = 4 if tcount % 4 == 0 else 1

    def several(i, carry):
        for k in range(group):
            visit(i * group + k)
        return carry

    if tcount == group:
        several(0, 0)
    else:
        lax.fori_loop(0, tcount // group, several, 0)


def localise_kernel(adjoint, side, n_gather, ntile_ref, nedge_ref, depart_ref, *refs):
    x_ref, given = refs[0], refs[1 : 1 + max(n_gather, 1)]
    out_ref, refs = refs[len(given) + 1], refs[len(given) + 2 :]
    gathered, refs = refs[:n_gather], refs[n_gather:]
    d_ref = gathered[0] if n_gather else given[0]
    xin, ystage, xs, es, gh, idx = refs[:6]
    in_send, in_recv, out_send, out_recv, side_send, side_recv, own_sem, side_own = refs[6:]
    tcount, pieces, _, lanes = xs.shape
    members, depth = xin.shape[1:3]
    pair = ROWS // depth
    blocks = members // pair
    low, left, right, corner, even = masks(side)
    me = lax.axis_index("tile")

    def peer_of(step):
        return lax.rem(me + step, tcount)

    def inward(block, step):
        rows = pl.ds(block * pair, pair)
        return pltpu.make_async_remote_copy(
            src_ref=x_ref.at[peer_of(step), rows],
            dst_ref=xin.at[me, rows],
            send_sem=in_send.at[block, step - 1],
            recv_sem=in_recv.at[block, step - 1],
            device_id={"tile": peer_of(step)},
            device_id_type=MESH,
        )

    def outward(block, step):
        rows = pl.ds(block * pair, pair)
        return pltpu.make_async_remote_copy(
            src_ref=ystage.at[peer_of(step), rows],
            dst_ref=out_ref.at[me, rows],
            send_sem=out_send.at[block, step - 1],
            recv_sem=out_recv.at[block, step - 1],
            device_id={"tile": peer_of(step)},
            device_id_type=MESH,
        )

    def sideways(which, step):
        return pltpu.make_async_remote_copy(
            src_ref=given[which],
            dst_ref=gathered[which].at[me],
            send_sem=side_send.at[which, step - 1],
            recv_sem=side_recv.at[which, step - 1],
            device_id={"tile": peer_of(step)},
            device_id_type=MESH,
        )

    barrier = pltpu.get_barrier_semaphore()
    for step in range(1, tcount):
        pl.semaphore_signal(
            barrier, inc=1, device_id={"tile": peer_of(step)}, device_id_type=MESH
        )
    own_in = pltpu.make_async_copy(x_ref.at[me], xin.at[me], own_sem.at[0])
    own_in.start()
    own_sides = [
        pltpu.make_async_copy(given[which], gathered[which].at[me], side_own.at[which])
        for which in range(n_gather)
    ]
    for copy in own_sides:
        copy.start()
    over_tiles(tcount, lambda tile: fill_index(nedge_ref, depart_ref, idx, tile, side))
    pl.semaphore_wait(barrier, tcount - 1)
    steps = range(1, tcount)
    for which in range(min(n_gather, 1)):
        for step in steps:
            sideways(which, step).start()
    for block in range(blocks):
        for step in steps:
            inward(block, step).start()
    for which in range(1, n_gather):
        for step in steps:
            sideways(which, step).start()
    for which in range(min(n_gather, 1)):
        own_sides[which].wait()
        for step in steps:
            sideways(which, step).wait()
    own_in.wait()

    def one_block(block, carry):
        for step in steps:
            inward(block, step).wait()

        def load(tile):
            columns = []
            for j in range(pieces):
                cells = slice(j * lanes, (j + 1) * lanes)
                x = jnp.concatenate(
                    [xin[tile, block * pair + m, :, cells] for m in range(pair)], axis=0
                )
                if adjoint:
                    x = x * d_ref[tile, :, cells]
                xs[tile, j] = x
                columns.append(column_part(x, j, corner, lanes))
                if j == 0:
                    first = x
            store_edges(es, tile, columns, first, x, low)

        over_tiles(tcount, load)

        def ghosts(tile):
            slots = [slot_of(ntile_ref, nedge_ref, tile, edge) for edge in range(4)]
            got = [es[slot] for slot in slots]
            row_idx, col_idx = idx[2 * tile + 1], idx[2 * tile]
            gh[2 * tile] = jnp.where(even, pick(got[2], col_idx), pick(got[3], col_idx))
            gh[2 * tile + 1] = jnp.where(low, pick(got[0], row_idx), pick(got[1], row_idx))

        def update(tile):
            cols, rows = gh[2 * tile], gh[2 * tile + 1]
            x = xs[tile, 0]
            before, here = rows, pltpu.roll(x, side, 1)
            columns = []
            for j in range(pieces):
                if j + 1 < pieces:
                    after_x = xs[tile, j + 1]
                    after = pltpu.roll(after_x, side, 1)
                else:
                    after_x, after = None, rows
                ghost = cols if j == 0 else pltpu.roll(cols, lanes - 2 * j, 1)
                total = here + jnp.where(low, before, after)
                total = total + jnp.where(left, ghost, pltpu.roll(x, 1, 1))
                total = total + jnp.where(right, ghost, pltpu.roll(x, lanes - 1, 1))
                rate = d_ref[tile, :, j * lanes : (j + 1) * lanes]
                new = x + rate * (total - 4.0 * x)
                xs[tile, j] = new
                columns.append(column_part(new, j, corner, lanes))
                if j == 0:
                    first = new
                x, before, here = after_x, here, after
            store_edges(es, tile, columns, first, new, low)

        def sweep(repeat, inner):
            over_tiles(tcount, ghosts)
            over_tiles(tcount, update)
            return inner

        lax.fori_loop(0, SWEEPS, sweep, 0)

        def store(tile):
            for j in range(pieces):
                cells = slice(j * lanes, (j + 1) * lanes)
                x = xs[tile, j]
                if adjoint:
                    x = x / d_ref[tile, :, cells]
                for m in range(pair):
                    ystage[tile, block * pair + m, :, cells] = x[m * depth : (m + 1) * depth]

        over_tiles(tcount, store)
        for step in steps:
            outward(block, step).start()
        return carry

    lax.fori_loop(0, blocks, one_block, 0)
    own_out = pltpu.make_async_copy(ystage.at[me], out_ref.at[me], own_sem.at[1])
    own_out.start()
    for which in range(1, n_gather):
        own_sides[which].wait()
        for step in steps:
            sideways(which, step).wait()
    own_out.wait()
    for block in range(blocks):
        for step in steps:
            outward(block, step).wait()


def localise(values, rate, gather, tables, side, tcount, adjoint, collective_id):
    _, members, depth, cells = values.shape
    lanes = 2 * side
    blocks = members * depth // ROWS
    smem = pl.BlockSpec(memory_space=pltpu.SMEM)
    vmem = pl.BlockSpec(memory_space=pltpu.VMEM)
    free = pl.BlockSpec(memory_space=pl.ANY)
    count = len(gather)
    shapes = [jax.ShapeDtypeStruct(values.shape, jnp.float32)]
    shapes += [jax.ShapeDtypeStruct((tcount,) + a.shape, a.dtype) for a in gather]
    others = max(tcount - 1, 1)
    sems = pltpu.SemaphoreType.DMA((blocks, others))
    side_sems = pltpu.SemaphoreType.DMA((max(count, 1), others))
    return pl.pallas_call(
        functools.partial(localise_kernel, adjoint, side, count),
        out_shape=shapes,
        in_specs=[smem] * 3 + [free] + ([free] * count if count else [vmem]),
        out_specs=[vmem] + ([vmem] + [free] * (count - 1) if count else []),
        scratch_shapes=[
            pltpu.VMEM(values.shape, jnp.float32),
            pltpu.VMEM(values.shape, jnp.float32),
            pltpu.VMEM((tcount, cells // lanes, ROWS, lanes), jnp.float32),
            pltpu.VMEM((2 * tcount, ROWS, lanes), jnp.float32),
            pltpu.VMEM((2 * tcount, ROWS, lanes), jnp.float32),
            pltpu.VMEM((2 * tcount, ROWS, lanes), jnp.int32),
            sems, sems, sems, sems, side_sems, side_sems,
            pltpu.SemaphoreType.DMA((2,)),
            pltpu.SemaphoreType.DMA((max(count, 1),)),
        ],
        compiler_params=pltpu.CompilerParams(
            collective_id=collective_id, has_side_effects=True, vmem_limit_bytes=VMEM_LIMIT
        ),
    )(*tables, values, *(gather if count else [rate]))


def transport_kernel(
    side, depth, mine_ref, ntile_ref, nedge_ref, depart_ref, flow_ref,
    x_ref, observed_ref, weight_ref, out_ref, xs, es, gh, idx, coef,
):
    tcount, pieces, _, lanes = xs.shape
    steps = flow_ref.shape[1]
    fields = x_ref.shape[1]
    low, left, right, corner, even = masks(side)
    row = lax.broadcasted_iota(jnp.int32, (ROWS, lanes), 0)
    level = lax.rem(mine_ref[0] * fields + lax.rem(row, fields), depth)

    def wide(ref, tile, cells):
        return jnp.concatenate([ref[tile, :, cells]] * (ROWS // fields), axis=0)

    def load(tile):
        fill_index(nedge_ref, depart_ref, idx, tile, side)
        for step in range(steps):
            rest = jnp.ones((ROWS, lanes), jnp.float32)
            for way in range(4):
                speed = jnp.zeros((ROWS, lanes), jnp.float32)
                for at in range(depth):
                    speed = jnp.where(level == at, flow_ref[tile, step, at, way], speed)
                coef[step, tile, way] = speed
                rest = rest - speed
            coef[step, tile, 4] = rest
        columns = []
        for j in range(pieces):
            x = wide(x_ref, tile, slice(j * lanes, (j + 1) * lanes))
            xs[tile, j] = x
            columns.append(column_part(x, j, corner, lanes))
            if j == 0:
                first = x
        store_edges(es, tile, columns, first, x, low)

    over_tiles(tcount, load)

    turns = [(s, False) for s in range(steps)] + [(s, True) for s in reversed(range(steps))]
    for turn, (step, adjoint) in enumerate(turns):

        def ghosts(tile, step=step, adjoint=adjoint):
            picked = []
            for edge in range(4):
                values = es[slot_of(ntile_ref, nedge_ref, tile, edge)]
                values = pick(values, idx[2 * tile + (1 if edge < 2 else 0)])
                if adjoint:
                    scale = coef[step, ntile_ref[tile, edge], nedge_ref[tile, edge]]
                else:
                    scale = coef[step, tile, edge]
                picked.append(values * scale)
            gh[2 * tile] = jnp.where(even, picked[2], picked[3])
            gh[2 * tile + 1] = jnp.where(low, picked[0], picked[1])

        def update(tile, turn=turn, step=step, adjoint=adjoint):
            cols, rows = gh[2 * tile], gh[2 * tile + 1]
            speeds = [coef[step, tile, way] for way in range(4)]
            if adjoint:
                speeds = [speeds[1], speeds[0], speeds[3], speeds[2]]
            rest = coef[step, tile, 4]
            x = xs[tile, 0]
            before, here = None, pltpu.roll(x, side, 1)
            columns = []
            for j in range(pieces):
                if j + 1 < pieces:
                    after_x = xs[tile, j + 1]
                    after = pltpu.roll(after_x, side, 1)
                    down = speeds[1] * jnp.where(low, here, after)
                else:
                    after_x, after = None, None
                    down = jnp.where(low, speeds[1] * here, rows)
                if j == 0:
                    up = jnp.where(low, rows, speeds[0] * here)
                else:
                    up = speeds[0] * jnp.where(low, before, here)
                ghost = cols if j == 0 else pltpu.roll(cols, lanes - 2 * j, 1)
                new = rest * x + up + down
                new = new + jnp.where(left, ghost, speeds[2] * pltpu.roll(x, 1, 1))
                new = new + jnp.where(right, ghost, speeds[3] * pltpu.roll(x, lanes - 1, 1))
                cells = slice(j * lanes, (j + 1) * lanes)
                if turn == steps - 1:
                    new = wide(weight_ref, tile, cells) * (new - wide(observed_ref, tile, cells))
                if turn == len(turns) - 1:
                    out_ref[tile, :, cells] = new[:fields]
                else:
                    xs[tile, j] = new
                    columns.append(column_part(new, j, corner, lanes))
                if j == 0:
                    first = new
                x, before, here = after_x, here, after
            if turn < len(turns) - 1:
                store_edges(es, tile, columns, first, new, low)

        over_tiles(tcount, ghosts)
        over_tiles(tcount, update)


def transport(states, observed, weight, flow, tables, mine, side, depth):
    tcount, fields, cells = states.shape
    lanes = 2 * side
    smem = pl.BlockSpec(memory_space=pltpu.SMEM)
    vmem = pl.BlockSpec(memory_space=pltpu.VMEM)
    return pl.pallas_call(
        functools.partial(transport_kernel, side, depth),
        out_shape=jax.ShapeDtypeStruct(states.shape, jnp.float32),
        in_specs=[smem] * 5 + [vmem] * 3,
        out_specs=vmem,
        scratch_shapes=[
            pltpu.VMEM((tcount, cells // lanes, ROWS, lanes), jnp.float32),
            pltpu.VMEM((2 * tcount, ROWS, lanes), jnp.float32),
            pltpu.VMEM((2 * tcount, ROWS, lanes), jnp.float32),
            pltpu.VMEM((2 * tcount, ROWS, lanes), jnp.int32),
            pltpu.VMEM((flow.shape[1], tcount, 5, ROWS, lanes), jnp.float32),
        ],
        compiler_params=pltpu.CompilerParams(vmem_limit_bytes=VMEM_LIMIT),
    )(mine, *tables, flow, states, observed, weight)


def body(
    mcount,
    tcount,
    control,
    perturbations,
    diffusivity,
    flow,
    observed,
    obs_weight,
    neighbour_tile,
    neighbour_edge,
    departure,
):
    members, _, depth, cells = control.shape
    kinds = perturbations.shape[2]
    side = departure.shape[-1]
    share = kinds * depth // mcount
    mine = lax.axis_index("member")
    tables = (neighbour_tile, neighbour_edge, departure)

    def own_fields(values):
        grouped = values.reshape(mcount, share, cells)
        return lax.dynamic_index_in_dim(grouped, mine, 0, keepdims=False)

    grouped = (tcount, members // tcount, depth, cells)
    smoothed, rate, flows, target, weight = localise(
        control.reshape(grouped), None,
        [diffusivity, flow[:, 0], own_fields(observed), own_fields(obs_weight)],
        tables, side, tcount, False, 1,
    )
    smoothed = smoothed.reshape(members, depth, cells)
    part = jnp.sum(perturbations[:, 0] * smoothed[:, None], axis=0)
    states = reduce_fields(part.reshape(mcount, share, cells), mcount, tcount, 3)
    sensitivity = transport(states, target, weight, flows, tables, mine.reshape(1), side, depth)
    sensitivity = spread_fields(sensitivity, mcount, 4).reshape(kinds, depth, cells)
    projected = jnp.sum(perturbations[:, 0] * sensitivity[None], axis=1)
    mixed = localise(projected.reshape(grouped), rate, [], tables, side, tcount, True, 2)[0]
    return control + mixed.reshape(control.shape)


def solution(mesh):
    in_specs = (
        P("member", "tile", None, None),
        P("member", "tile", None, None, None),
        P("tile", None),
        P(None, "tile", None, None),
        P("tile", None, None, None),
        P("tile", None, None, None),
        P(),
        P(),
        P(),
    )
    out_specs = P("member", "tile", None, None)
    run = functools.partial(body, mesh.shape["member"], mesh.shape["tile"])
    return jax.shard_map(run, mesh=mesh, in_specs=in_specs, out_specs=out_specs, check_vma=False)
```

```python
import functools

import jax
import jax.numpy as jnp
from jax import lax
from jax.experimental import pallas as pl
from jax.experimental.pallas import tpu as pltpu
from jax.sharding import PartitionSpec as P

SWEEPS = 8
ROWS = 8
MESH = pl.DeviceIdType.MESH
VMEM_LIMIT = 40 * 1024 * 1024


def reduce_kernel(mcount, tcount, part_ref, out_ref, landed, msend, mrecv, tsend, trecv):
    mine = lax.axis_index("member")
    here = lax.axis_index("tile")
    barrier = pltpu.get_barrier_semaphore()
    for step in range(1, mcount):
        pl.semaphore_signal(
            barrier, inc=1, device_id={"member": lax.rem(mine + step, mcount)}, device_id_type=MESH
        )
    for step in range(1, tcount):
        pl.semaphore_signal(
            barrier, inc=1, device_id={"tile": lax.rem(here + step, tcount)}, device_id_type=MESH
        )
    pl.semaphore_wait(barrier, mcount + tcount - 2)
    copies = []
    for step in range(1, mcount):
        peer = lax.rem(mine + step, mcount)
        copy = pltpu.make_async_remote_copy(
            src_ref=part_ref.at[peer],
            dst_ref=landed.at[step - 1],
            send_sem=msend.at[step - 1],
            recv_sem=mrecv.at[step - 1],
            device_id={"member": peer},
            device_id_type=MESH,
        )
        copy.start()
        copies.append(copy)
    for copy in copies:
        copy.wait()
    total = part_ref[mine]
    for step in range(1, mcount):
        total = total + landed[step - 1]
    out_ref[here] = total
    copies = []
    for step in range(1, tcount):
        copy = pltpu.make_async_remote_copy(
            src_ref=out_ref.at[here],
            dst_ref=out_ref.at[here],
            send_sem=tsend.at[step - 1],
            recv_sem=trecv.at[step - 1],
            device_id={"tile": lax.rem(here + step, tcount)},
            device_id_type=MESH,
        )
        copy.start()
        copies.append(copy)
    for copy in copies:
        copy.wait()


def reduce_fields(part, mcount, tcount, collective_id):
    block = part.shape[1:]
    return pl.pallas_call(
        functools.partial(reduce_kernel, mcount, tcount),
        out_shape=jax.ShapeDtypeStruct((tcount,) + block, jnp.float32),
        in_specs=[pl.BlockSpec(memory_space=pltpu.VMEM)],
        out_specs=pl.BlockSpec(memory_space=pltpu.VMEM),
        scratch_shapes=[
            pltpu.VMEM((max(mcount - 1, 1),) + block, jnp.float32),
            pltpu.SemaphoreType.DMA((max(mcount - 1, 1),)),
            pltpu.SemaphoreType.DMA((max(mcount - 1, 1),)),
            pltpu.SemaphoreType.DMA((max(tcount - 1, 1),)),
            pltpu.SemaphoreType.DMA((max(tcount - 1, 1),)),
        ],
        compiler_params=pltpu.CompilerParams(
            collective_id=collective_id, has_side_effects=True, vmem_limit_bytes=VMEM_LIMIT
        ),
    )(part)


def spread_kernel(mcount, own_ref, out_ref, msend, mrecv):
    mine = lax.axis_index("member")
    here = lax.axis_index("tile")
    barrier = pltpu.get_barrier_semaphore()
    for step in range(1, mcount):
        pl.semaphore_signal(
            barrier, inc=1, device_id={"member": lax.rem(mine + step, mcount)}, device_id_type=MESH
        )
    pl.semaphore_wait(barrier, mcount - 1)
    copies = []
    for step in range(1, mcount):
        copy = pltpu.make_async_remote_copy(
            src_ref=own_ref.at[here],
            dst_ref=out_ref.at[mine],
            send_sem=msend.at[step - 1],
            recv_sem=mrecv.at[step - 1],
            device_id={"member": lax.rem(mine + step, mcount)},
            device_id_type=MESH,
        )
        copy.start()
        copies.append(copy)
    out_ref[mine] = own_ref[here]
    for copy in copies:
        copy.wait()


def spread_fields(fields, mcount, collective_id):
    return pl.pallas_call(
        functools.partial(spread_kernel, mcount),
        out_shape=jax.ShapeDtypeStruct((mcount,) + fields.shape[1:], jnp.float32),
        in_specs=[pl.BlockSpec(memory_space=pltpu.VMEM)],
        out_specs=pl.BlockSpec(memory_space=pltpu.VMEM),
        scratch_shapes=[
            pltpu.SemaphoreType.DMA((max(mcount - 1, 1),)),
            pltpu.SemaphoreType.DMA((max(mcount - 1, 1),)),
        ],
        compiler_params=pltpu.CompilerParams(
            collective_id=collective_id, has_side_effects=True, vmem_limit_bytes=VMEM_LIMIT
        ),
    )(fields)


def lane_grid(lanes):
    return lax.broadcasted_iota(jnp.int32, (ROWS, lanes), 1)


def lane_of(edge, position, side):
    lanes = 2 * side
    column = side * (position & 1) + (position - (position & 1))
    column = column + jnp.where(edge == 3, side - 1, 0)
    column = jnp.where(column >= lanes, column - lanes, column)
    return jnp.where(edge < 2, position + side * edge, column)


def fill_index(nedge_ref, depart_ref, idx, tile, side):
    lanes = 2 * side
    lane = lane_grid(lanes)

    def source(pair, first, position):
        edge = jnp.where(first, nedge_ref[tile, pair], nedge_ref[tile, pair + 1])
        flip = jnp.where(first, depart_ref[tile, pair, 0], depart_ref[tile, pair + 1, 0])
        position = jnp.where(flip != 0, side - 1 - position, position)
        return lane_of(edge, position, side)

    low = lane < side
    idx[2 * tile + 1] = source(0, low, jnp.where(low, lane, lane - side))
    even = (lane & 1) == 0
    base = jnp.where(even, lane, (lane + side + 1) & (lanes - 1))
    upper = base >= side
    position = jnp.where(upper, base - side + 1, base)
    idx[2 * tile] = source(2, even, position)


def slot_of(ntile_ref, nedge_ref, tile, edge):
    return 2 * ntile_ref[tile, edge] + jnp.where(nedge_ref[tile, edge] < 2, 1, 0)


def pick(values, index):
    return jnp.take_along_axis(values, index, axis=1, mode="promise_in_bounds")


def column_part(piece, j, corner, lanes):
    kept = jnp.where(corner, piece, 0.0)
    return kept if j == 0 else pltpu.roll(kept, 2 * j, 1)


def store_edges(es, tile, columns, first, last, low):
    while len(columns) > 1:
        columns = [sum(columns[i : i + 2]) for i in range(0, len(columns), 2)]
    es[2 * tile] = columns[0]
    es[2 * tile + 1] = jnp.where(low, first, last)


def masks(side):
    lanes = 2 * side
    lane = lane_grid(lanes)
    low = lane < side
    left = (lane & (side - 1)) == 0
    right = (lane & (side - 1)) == side - 1
    return low, left, right, left | right, (lane & 1) == 0


def over_tiles(tcount, visit, group=1):
    group = group if tcount % group == 0 else 1

    def several(i, carry):
        for k in range(group):
            visit(i * group + k)
        return carry

    if tcount == group:
        several(0, 0)
    else:
        lax.fori_loop(0, tcount // group, several, 0)


def localise_kernel(adjoint, side, n_gather, ntile_ref, nedge_ref, depart_ref, *refs):
    x_ref, given = refs[0], refs[1 : 1 + max(n_gather, 1)]
    out_ref, refs = refs[len(given) + 1], refs[len(given) + 2 :]
    gathered, refs = refs[:n_gather], refs[n_gather:]
    d_ref = gathered[0] if n_gather else given[0]
    xin, ystage, xs, es, gh, idx = refs[:6]
    in_send, in_recv, out_send, out_recv, side_send, side_recv, own_sem, side_own = refs[6:]
    tcount, pieces, _, lanes = xs.shape
    members, depth = xin.shape[1:3]
    pair = ROWS // depth
    blocks = members // pair
    low, left, right, corner, even = masks(side)
    me = lax.axis_index("tile")

    def peer_of(step):
        return lax.rem(me + step, tcount)

    def inward(block, step):
        rows = pl.ds(block * pair, pair)
        return pltpu.make_async_remote_copy(
            src_ref=x_ref.at[peer_of(step), rows],
            dst_ref=xin.at[me, rows],
            send_sem=in_send.at[block, step - 1],
            recv_sem=in_recv.at[block, step - 1],
            device_id={"tile": peer_of(step)},
            device_id_type=MESH,
        )

    def outward(block, step):
        rows = pl.ds(block * pair, pair)
        return pltpu.make_async_remote_copy(
            src_ref=ystage.at[peer_of(step), rows],
            dst_ref=out_ref.at[me, rows],
            send_sem=out_send.at[block, step - 1],
            recv_sem=out_recv.at[block, step - 1],
            device_id={"tile": peer_of(step)},
            device_id_type=MESH,
        )

    def sideways(which, step):
        return pltpu.make_async_remote_copy(
            src_ref=given[which],
            dst_ref=gathered[which].at[me],
            send_sem=side_send.at[which, step - 1],
            recv_sem=side_recv.at[which, step - 1],
            device_id={"tile": peer_of(step)},
            device_id_type=MESH,
        )

    barrier = pltpu.get_barrier_semaphore()
    for step in range(1, tcount):
        pl.semaphore_signal(
            barrier, inc=1, device_id={"tile": peer_of(step)}, device_id_type=MESH
        )
    own_in = pltpu.make_async_copy(x_ref.at[me], xin.at[me], own_sem.at[0])
    own_in.start()
    own_sides = [
        pltpu.make_async_copy(given[which], gathered[which].at[me], side_own.at[which])
        for which in range(n_gather)
    ]
    for copy in own_sides:
        copy.start()
    over_tiles(tcount, lambda tile: fill_index(nedge_ref, depart_ref, idx, tile, side))
    pl.semaphore_wait(barrier, tcount - 1)
    steps = range(1, tcount)
    for which in range(min(n_gather, 1)):
        for step in steps:
            sideways(which, step).start()
    for block in range(blocks):
        for step in steps:
            inward(block, step).start()
    for which in range(1, n_gather):
        for step in steps:
            sideways(which, step).start()
    for which in range(min(n_gather, 1)):
        own_sides[which].wait()
        for step in steps:
            sideways(which, step).wait()
    own_in.wait()

    def one_block(block, carry):
        for step in steps:
            inward(block, step).wait()

        def load(tile):
            columns = []
            for j in range(pieces):
                cells = slice(j * lanes, (j + 1) * lanes)
                x = jnp.concatenate(
                    [xin[tile, block * pair + m, :, cells] for m in range(pair)], axis=0
                )
                if adjoint:
                    x = x * d_ref[tile, :, cells]
                xs[tile, j] = x
                columns.append(column_part(x, j, corner, lanes))
                if j == 0:
                    first = x
            store_edges(es, tile, columns, first, x, low)

        over_tiles(tcount, load)

        def ghosts(tile):
            slots = [slot_of(ntile_ref, nedge_ref, tile, edge) for edge in range(4)]
            got = [es[slot] for slot in slots]
            row_idx, col_idx = idx[2 * tile + 1], idx[2 * tile]
            gh[2 * tile] = jnp.where(even, pick(got[2], col_idx), pick(got[3], col_idx))
            gh[2 * tile + 1] = jnp.where(low, pick(got[0], row_idx), pick(got[1], row_idx))

        def update(tile):
            cols, rows = gh[2 * tile], gh[2 * tile + 1]
            x = xs[tile, 0]
            before, here = rows, pltpu.roll(x, side, 1)
            columns = []
            for j in range(pieces):
                if j + 1 < pieces:
                    after_x = xs[tile, j + 1]
                    after = pltpu.roll(after_x, side, 1)
                else:
                    after_x, after = None, rows
                ghost = cols if j == 0 else pltpu.roll(cols, lanes - 2 * j, 1)
                total = here + jnp.where(low, before, after)
                total = total + jnp.where(left, ghost, pltpu.roll(x, 1, 1))
                total = total + jnp.where(right, ghost, pltpu.roll(x, lanes - 1, 1))
                rate = d_ref[tile, :, j * lanes : (j + 1) * lanes]
                new = x + rate * (total - 4.0 * x)
                xs[tile, j] = new
                columns.append(column_part(new, j, corner, lanes))
                if j == 0:
                    first = new
                x, before, here = after_x, here, after
            store_edges(es, tile, columns, first, new, low)

        def sweep(repeat, inner):
            over_tiles(tcount, ghosts, 4)
            over_tiles(tcount, update)
            return inner

        lax.fori_loop(0, SWEEPS, sweep, 0)

        def store(tile):
            for j in range(pieces):
                cells = slice(j * lanes, (j + 1) * lanes)
                x = xs[tile, j]
                if adjoint:
                    x = x / d_ref[tile, :, cells]
                for m in range(pair):
                    ystage[tile, block * pair + m, :, cells] = x[m * depth : (m + 1) * depth]

        over_tiles(tcount, store)
        for step in steps:
            outward(block, step).start()
        return carry

    lax.fori_loop(0, blocks, one_block, 0)
    own_out = pltpu.make_async_copy(ystage.at[me], out_ref.at[me], own_sem.at[1])
    own_out.start()
    for which in range(1, n_gather):
        own_sides[which].wait()
        for step in steps:
            sideways(which, step).wait()
    own_out.wait()
    for block in range(blocks):
        for step in steps:
            outward(block, step).wait()


def localise(values, rate, gather, tables, side, tcount, adjoint, collective_id):
    _, members, depth, cells = values.shape
    lanes = 2 * side
    blocks = members * depth // ROWS
    smem = pl.BlockSpec(memory_space=pltpu.SMEM)
    vmem = pl.BlockSpec(memory_space=pltpu.VMEM)
    free = pl.BlockSpec(memory_space=pl.ANY)
    count = len(gather)
    shapes = [jax.ShapeDtypeStruct(values.shape, jnp.float32)]
    shapes += [jax.ShapeDtypeStruct((tcount,) + a.shape, a.dtype) for a in gather]
    others = max(tcount - 1, 1)
    sems = pltpu.SemaphoreType.DMA((blocks, others))
    side_sems = pltpu.SemaphoreType.DMA((max(count, 1), others))
    return pl.pallas_call(
        functools.partial(localise_kernel, adjoint, side, count),
        out_shape=shapes,
        in_specs=[smem] * 3 + [free] + ([free] * count if count else [vmem]),
        out_specs=[vmem] + ([vmem] + [free] * (count - 1) if count else []),
        scratch_shapes=[
            pltpu.VMEM(values.shape, jnp.float32),
            pltpu.VMEM(values.shape, jnp.float32),
            pltpu.VMEM((tcount, cells // lanes, ROWS, lanes), jnp.float32),
            pltpu.VMEM((2 * tcount, ROWS, lanes), jnp.float32),
            pltpu.VMEM((2 * tcount, ROWS, lanes), jnp.float32),
            pltpu.VMEM((2 * tcount, ROWS, lanes), jnp.int32),
            sems, sems, sems, sems, side_sems, side_sems,
            pltpu.SemaphoreType.DMA((2,)),
            pltpu.SemaphoreType.DMA((max(count, 1),)),
        ],
        compiler_params=pltpu.CompilerParams(
            collective_id=collective_id, has_side_effects=True, vmem_limit_bytes=VMEM_LIMIT
        ),
    )(*tables, values, *(gather if count else [rate]))


def transport_kernel(
    side, depth, mine_ref, ntile_ref, nedge_ref, depart_ref, flow_ref,
    x_ref, observed_ref, weight_ref, out_ref, xs, es, gh, idx, coef,
):
    tcount, pieces, _, lanes = xs.shape
    steps = flow_ref.shape[1]
    fields = x_ref.shape[1]
    low, left, right, corner, even = masks(side)
    row = lax.broadcasted_iota(jnp.int32, (ROWS, lanes), 0)
    level = lax.rem(mine_ref[0] * fields + lax.rem(row, fields), depth)

    def wide(ref, tile, cells):
        return jnp.concatenate([ref[tile, :, cells]] * (ROWS // fields), axis=0)

    def load(tile):
        fill_index(nedge_ref, depart_ref, idx, tile, side)
        for step in range(steps):
            rest = jnp.ones((ROWS, lanes), jnp.float32)
            for way in range(4):
                speed = jnp.zeros((ROWS, lanes), jnp.float32)
                for at in range(depth):
                    speed = jnp.where(level == at, flow_ref[tile, step, at, way], speed)
                coef[step, tile, way] = speed
                rest = rest - speed
            coef[step, tile, 4] = rest
        columns = []
        for j in range(pieces):
            x = wide(x_ref, tile, slice(j * lanes, (j + 1) * lanes))
            xs[tile, j] = x
            columns.append(column_part(x, j, corner, lanes))
            if j == 0:
                first = x
        store_edges(es, tile, columns, first, x, low)

    over_tiles(tcount, load)

    turns = [(s, False) for s in range(steps)] + [(s, True) for s in reversed(range(steps))]
    for turn, (step, adjoint) in enumerate(turns):

        def ghosts(tile, step=step, adjoint=adjoint):
            picked = []
            for edge in range(4):
                values = es[slot_of(ntile_ref, nedge_ref, tile, edge)]
                values = pick(values, idx[2 * tile + (1 if edge < 2 else 0)])
                if adjoint:
                    scale = coef[step, ntile_ref[tile, edge], nedge_ref[tile, edge]]
                else:
                    scale = coef[step, tile, edge]
                picked.append(values * scale)
            gh[2 * tile] = jnp.where(even, picked[2], picked[3])
            gh[2 * tile + 1] = jnp.where(low, picked[0], picked[1])

        def update(tile, turn=turn, step=step, adjoint=adjoint):
            cols, rows = gh[2 * tile], gh[2 * tile + 1]
            speeds = [coef[step, tile, way] for way in range(4)]
            if adjoint:
                speeds = [speeds[1], speeds[0], speeds[3], speeds[2]]
            rest = coef[step, tile, 4]
            x = xs[tile, 0]
            before, here = None, pltpu.roll(x, side, 1)
            columns = []
            for j in range(pieces):
                if j + 1 < pieces:
                    after_x = xs[tile, j + 1]
                    after = pltpu.roll(after_x, side, 1)
                    down = speeds[1] * jnp.where(low, here, after)
                else:
                    after_x, after = None, None
                    down = jnp.where(low, speeds[1] * here, rows)
                if j == 0:
                    up = jnp.where(low, rows, speeds[0] * here)
                else:
                    up = speeds[0] * jnp.where(low, before, here)
                ghost = cols if j == 0 else pltpu.roll(cols, lanes - 2 * j, 1)
                new = rest * x + up + down
                new = new + jnp.where(left, ghost, speeds[2] * pltpu.roll(x, 1, 1))
                new = new + jnp.where(right, ghost, speeds[3] * pltpu.roll(x, lanes - 1, 1))
                cells = slice(j * lanes, (j + 1) * lanes)
                if turn == steps - 1:
                    new = wide(weight_ref, tile, cells) * (new - wide(observed_ref, tile, cells))
                if turn == len(turns) - 1:
                    out_ref[tile, :, cells] = new[:fields]
                else:
                    xs[tile, j] = new
                    columns.append(column_part(new, j, corner, lanes))
                if j == 0:
                    first = new
                x, before, here = after_x, here, after
            if turn < len(turns) - 1:
                store_edges(es, tile, columns, first, new, low)

        over_tiles(tcount, ghosts, 4)
        over_tiles(tcount, update)


def transport(states, observed, weight, flow, tables, mine, side, depth):
    tcount, fields, cells = states.shape
    lanes = 2 * side
    smem = pl.BlockSpec(memory_space=pltpu.SMEM)
    vmem = pl.BlockSpec(memory_space=pltpu.VMEM)
    return pl.pallas_call(
        functools.partial(transport_kernel, side, depth),
        out_shape=jax.ShapeDtypeStruct(states.shape, jnp.float32),
        in_specs=[smem] * 5 + [vmem] * 3,
        out_specs=vmem,
        scratch_shapes=[
            pltpu.VMEM((tcount, cells // lanes, ROWS, lanes), jnp.float32),
            pltpu.VMEM((2 * tcount, ROWS, lanes), jnp.float32),
            pltpu.VMEM((2 * tcount, ROWS, lanes), jnp.float32),
            pltpu.VMEM((2 * tcount, ROWS, lanes), jnp.int32),
            pltpu.VMEM((flow.shape[1], tcount, 5, ROWS, lanes), jnp.float32),
        ],
        compiler_params=pltpu.CompilerParams(vmem_limit_bytes=VMEM_LIMIT),
    )(mine, *tables, flow, states, observed, weight)


def body(
    mcount,
    tcount,
    control,
    perturbations,
    diffusivity,
    flow,
    observed,
    obs_weight,
    neighbour_tile,
    neighbour_edge,
    departure,
):
    members, _, depth, cells = control.shape
    kinds = perturbations.shape[2]
    side = departure.shape[-1]
    share = kinds * depth // mcount
    mine = lax.axis_index("member")
    tables = (neighbour_tile, neighbour_edge, departure)

    def own_fields(values):
        grouped = values.reshape(mcount, share, cells)
        return lax.dynamic_index_in_dim(grouped, mine, 0, keepdims=False)

    grouped = (tcount, members // tcount, depth, cells)
    smoothed, rate, flows, target, weight = localise(
        control.reshape(grouped), None,
        [diffusivity, flow[:, 0], own_fields(observed), own_fields(obs_weight)],
        tables, side, tcount, False, 1,
    )
    smoothed = smoothed.reshape(members, depth, cells)
    part = jnp.sum(perturbations[:, 0] * smoothed[:, None], axis=0)
    states = reduce_fields(part.reshape(mcount, share, cells), mcount, tcount, 3)
    sensitivity = transport(states, target, weight, flows, tables, mine.reshape(1), side, depth)
    sensitivity = spread_fields(sensitivity, mcount, 4).reshape(kinds, depth, cells)
    projected = jnp.sum(perturbations[:, 0] * sensitivity[None], axis=1)
    mixed = localise(projected.reshape(grouped), rate, [], tables, side, tcount, True, 2)[0]
    return control + mixed.reshape(control.shape)


def solution(mesh):
    in_specs = (
        P("member", "tile", None, None),
        P("member", "tile", None, None, None),
        P("tile", None),
        P(None, "tile", None, None),
        P("tile", None, None, None),
        P("tile", None, None, None),
        P(),
        P(),
        P(),
    )
    out_specs = P("member", "tile", None, None)
    run = functools.partial(body, mesh.shape["member"], mesh.shape["tile"])
    return jax.shard_map(run, mesh=mesh, in_specs=in_specs, out_specs=out_specs, check_vma=False)
```
